32 devices in a mesh: tp: 2 (over core), row: 4 (over y, x), col: 4 (over z).
Axes of the slice: x: 2, y: 2, z: 4, core: 2. Of those that a mesh axis runs over, the one named last changes fastest.
Arguments:
- acts: bfloat16 [128, 128, 4096], P(('row', 'col'), None, 'tp'), may hold values from -6 to 6
- grads: bfloat16 [128, 128, 4096], P(('row', 'col'), None, 'tp'), may hold values from -6 to 6
- proj_in: bfloat16 [4096, 192], P('tp'), may hold values from -0.09375 to 0.09375
- proj_out: bfloat16 [4096, 64], P('tp'), may hold values from -0.09375 to 0.09375
- curvature: float32 [12288, 12288], P('row', ('tp', 'col')), may hold values from -1 to 7, as said below
Outputs:
- trailing: float32 [12288, 12288], P('row', ('tp', 'col'))
- panel: float32 [12288, 512], P('row', 'tp')
The draws below stay inside these ranges and needn't reach their ends.
Inputs may be any that keep to these rules, and one draw needn't show every extreme that they name: curvature is symmetric.
All inputs are finite; a program needn't handle non-finite values.
Results may differ from the reference program's by a relative error of at most 0.0021.
Values may be sent and summed in bfloat16 or wider, within the bound.
A program may use at most 128 MiB of HBM per device.

```python
import jax
import jax.numpy as jnp
from jax import lax

D = 4096
KA = 192
KG = 64
PANEL = 512
SEQ = 128
ORDER = 12288
EXAMPLES = 128


def draw_curvature(key, part):
    base = jax.random.fold_in(key, 31)
    noise_key, diag_key = jax.random.split(base)
    index = jnp.arange(ORDER, dtype=jnp.float32)
    distance = jnp.abs(index[:, None] - index[None, :])
    noise = jax.random.truncated_normal(noise_key, -4.0, 4.0, (ORDER, ORDER), jnp.float32)
    levels = jax.random.uniform(diag_key, (ORDER,), jnp.float32)
    reach = 64.0
    spread = (0.5 / ORDER) ** 0.5
    symmetric = (noise + noise.T) * spread
    coupled = 5.0 * jnp.exp(-distance / reach)
    return symmetric + coupled + jnp.diag(0.5 + levels)


def block_levels(rng, dims, shards, low, top_value):
    level, own = 1.0, jax.random.fold_in(rng, 6)
    for position, shards_of in shards:
        draws = jnp.exp(jax.random.uniform(jax.random.fold_in(own, position), (shards_of,), jnp.float32, low / len(shards), top_value / len(shards)))
        level = level * jnp.repeat(draws, dims[position] // shards_of).reshape([-1 if axis == position else 1 for axis in range(len(dims))])
    return level


def normal_values(key, shape, deviation, most, cuts=(), held_as=jnp.bfloat16):
    result = deviation * jax.random.normal(key, shape, jnp.float32)
    if cuts:
        result = result * block_levels(key, shape, cuts, -0.22, 0.18)
    return jnp.clip(result, -most, most).astype(held_as)


def setup_inputs(seed: int = 0) -> dict:
    key_of = jax.random.split(jax.random.key(seed), 6)
    acts = normal_values(key_of[0], (EXAMPLES, SEQ, D), 1.0, 6.0, ((0, 16), (2, 2)))
    grads = normal_values(key_of[1], (EXAMPLES, SEQ, D), 1.0, 6.0, ((0, 16), (2, 2)))
    proj_in = normal_values(key_of[2], (D, KA), D ** -0.5, 0.09375, ((0, 2),))
    proj_out = normal_values(key_of[3], (D, KG), D ** -0.5, 0.09375, ((0, 2),))
    curvature = draw_curvature(jax.random.fold_in(key_of[5], 71), 0)
    return dict(acts=acts, grads=grads, proj_in=proj_in, proj_out=proj_out, curvature=curvature)


def reference(acts, grads, proj_in, proj_out, curvature):
    examples, seq_len, width = acts.shape
    scale = (seq_len * examples) ** (-0.5)
    proj_acts = jnp.dot(acts.reshape(-1, width).astype(jnp.float32), proj_in.astype(jnp.float32), preferred_element_type=jnp.float32).reshape(examples, seq_len, -1)
    proj_grads = jnp.dot(grads.reshape(-1, width).astype(jnp.float32), proj_out.astype(jnp.float32), preferred_element_type=jnp.float32).reshape(examples, seq_len, -1)
    outer = jnp.einsum('nsi,nsj->nij', proj_acts, proj_grads, precision=lax.Precision.HIGHEST) * scale
    features = outer.reshape(examples, -1).astype(jnp.bfloat16)
    updated = curvature + jnp.dot(features.T.astype(jnp.float32), features.astype(jnp.float32), preferred_element_type=jnp.float32)
    diag_factor = jnp.linalg.cholesky(updated[:PANEL, :PANEL])
    panel = jax.scipy.linalg.solve_triangular(diag_factor, updated[:, :PANEL].T, lower=True).T
    trailing = updated - jnp.dot(panel.astype(jnp.float32), panel.T.astype(jnp.float32), precision=lax.Precision.HIGHEST, preferred_element_type=jnp.float32)
    return (trailing, panel)
```

```python
import functools

import jax
import jax.numpy as jnp
from jax import lax
from jax.experimental import pallas as pl
from jax.experimental.pallas import tpu as pltpu
from jax.sharding import PartitionSpec as P

PANEL = 512
NB = 128
precise = lax.Precision.HIGHEST


def factor_block(s, w):
    n = len(s)
    sub = lax.broadcasted_iota(jnp.int32, (8, NB), 0)
    s, w = list(s), list(w)
    for q in range(n):
        c = [
            [jnp.broadcast_to(s[i][:, 8 * q + j : 8 * q + j + 1], (8, NB)) for j in range(8)]
            for i in range(q, n)
        ]
        scale = jnp.zeros((8, NB), jnp.float32)
        for r in range(8):
            piv = jnp.broadcast_to(c[0][r][r : r + 1], (8, NB))
            inv = 1.0 / piv
            scale = jnp.where(sub == r, lax.rsqrt(piv), scale)
            row_s = jnp.broadcast_to(s[q][r : r + 1], (8, NB)) * inv
            row_w = jnp.broadcast_to(w[q][r : r + 1], (8, NB)) * inv
            row_c = [None] * 8
            for j in range(r + 1, 8):
                row_c[j] = jnp.broadcast_to(c[0][j][r : r + 1], (8, NB)) * inv
            for i in range(q, n):
                m = c[i - q][r]
                if i == q:
                    m = jnp.where(sub > r, m, 0.0)
                s[i] = s[i] - m * row_s
                w[i] = w[i] - m * row_w
                for j in range(r + 1, 8):
                    c[i - q][j] = c[i - q][j] - m * row_c[j]
        s[q] = s[q] * scale
        w[q] = w[q] * scale
    return s, w


def inverse_kernel(a_ref, out_ref, work):
    n = a_ref.shape[0]
    row = lax.broadcasted_iota(jnp.int32, (n, n), 0)
    col = lax.broadcasted_iota(jnp.int32, (n, n), 1)
    work[:, :n] = a_ref[...]
    work[:, n:] = jnp.where(row == col, 1.0, 0.0)
    eye = [
        jnp.where(
            lax.broadcasted_iota(jnp.int32, (8, NB), 0) + 8 * i
            == lax.broadcasted_iota(jnp.int32, (8, NB), 1),
            1.0,
            0.0,
        )
        for i in range(NB // 8)
    ]

    for b in range(n // NB):
        lo = b * NB
        s = [work[lo + 8 * i : lo + 8 * i + 8, lo : lo + NB] for i in range(NB // 8)]
        _, t = factor_block(s, eye)
        t = jnp.concatenate(t, axis=0)
        full = jnp.dot(
            t, work[lo : lo + NB, :], precision=precise, preferred_element_type=jnp.float32
        )
        work[lo : lo + NB, :] = full
        if lo + NB < n:
            left = full[:, lo + NB : n]
            work[lo + NB :, :] -= lax.dot_general(
                left,
                full,
                (((0,), (0,)), ((), ())),
                precision=precise,
                preferred_element_type=jnp.float32,
            )
    out_ref[...] = jnp.where(row >= col, work[:, n:], 0.0)


def factor_inverse(a):
    n = a.shape[0]
    return pl.pallas_call(
        inverse_kernel,
        out_shape=jax.ShapeDtypeStruct((n, n), jnp.float32),
        in_specs=[pl.BlockSpec(memory_space=pltpu.VMEM)],
        out_specs=pl.BlockSpec(memory_space=pltpu.VMEM),
        scratch_shapes=[pltpu.VMEM((n, 2 * n), jnp.float32)],
        cost_estimate=pl.CostEstimate(
            flops=40_000_000_000, bytes_accessed=8 * n * n, transcendentals=0
        ),
        compiler_params=pltpu.CompilerParams(vmem_limit_bytes=32 << 20),
    )(a)


def per_device(acts, grads, proj_in, proj_out, curvature):
    tp_count = lax.axis_size("tp")
    row_count = lax.axis_size("row")
    col_count = lax.axis_size("col")
    tp_index = lax.axis_index("tp")
    row_index = lax.axis_index("row")
    col_index = lax.axis_index("col")
    ex_dev, seq_len, width = acts.shape
    rows_blk, cols_blk = curvature.shape
    act_width = proj_in.shape[1]
    grad_width = proj_out.shape[1]
    examples = ex_dev * row_count * col_count
    scale = (seq_len * examples) ** (-0.5)
    panel_w = PANEL
    block_index = tp_index * col_count + col_index

    zero = jnp.zeros((), jnp.float32)
    first_col = block_index == 0
    first_row = row_index == 0
    diag_raw = lax.psum(
        jnp.where(first_col & first_row, curvature[:panel_w, :panel_w], zero),
        ("tp", "row", "col"),
    )
    rows_raw = lax.psum(
        jnp.where(first_col, curvature[:, :panel_w], zero), ("tp", "col")
    )
    top_raw = lax.psum(jnp.where(first_row, curvature[:panel_w], zero), "row")

    act_part = jnp.dot(
        acts.reshape(-1, width), proj_in, preferred_element_type=jnp.float32
    ).reshape(ex_dev, seq_len, act_width)
    grad_part = jnp.dot(
        grads.reshape(-1, width), proj_out, preferred_element_type=jnp.float32
    ).reshape(ex_dev, seq_len, grad_width)
    proj_acts, proj_grads = lax.psum((act_part, grad_part), "tp")
    half = act_width // tp_count
    mine = lax.dynamic_slice_in_dim(proj_acts, tp_index * half, half, 2)
    local = (
        jnp.einsum("esi,esj->eij", mine, proj_grads, precision=precise) * scale
    ).astype(jnp.bfloat16)
    local = local.reshape(ex_dev, half * grad_width)
    feats = lax.all_gather(local, ("tp", "row", "col"), axis=0)
    feats = feats.reshape(tp_count, examples, half * grad_width)

    def part(start, size):
        per = half * grad_width
        if size <= per and per % size == 0:
            one = lax.dynamic_slice(
                feats, (start // per, 0, start % per), (1, examples, size)
            )
            return one[0]
        flat = jnp.concatenate([feats[t] for t in range(tp_count)], axis=1)
        return lax.dynamic_slice_in_dim(flat, start, size, 1)

    f_rows = part(row_index * rows_blk, rows_blk)
    f_cols = part(block_index * cols_blk, cols_blk)
    f_pan = feats[0][:, :panel_w]

    def gram(a, b):
        return lax.dot_general(
            a, b, (((0,), (0,)), ((), ())), preferred_element_type=jnp.float32
        )

    inverse = factor_inverse(diag_raw + gram(f_pan, f_pan))
    rows_upd = rows_raw + gram(f_rows, f_pan)
    top_upd = top_raw + gram(f_pan, f_cols)
    panel_rows = lax.dot_general(
        rows_upd,
        inverse,
        (((1,), (1,)), ((), ())),
        precision=precise,
        preferred_element_type=jnp.float32,
    )
    top_factor = jnp.dot(
        inverse, top_upd, precision=precise, preferred_element_type=jnp.float32
    )
    trailing = (curvature + gram(f_rows, f_cols)) - jnp.dot(
        panel_rows,
        top_factor,
        precision=lax.Precision.HIGH,
        preferred_element_type=jnp.float32,
    )
    width_out = panel_w // tp_count
    panel = lax.dynamic_slice_in_dim(panel_rows, tp_index * width_out, width_out, 1)
    return (trailing, panel)


def solution(mesh):
    in_specs = (
        P(("row", "col"), None, "tp"),
        P(("row", "col"), None, "tp"),
        P("tp", None),
        P("tp", None),
        P("row", ("tp", "col")),
    )
    out_specs = (P("row", ("tp", "col")), P("row", "tp"))
    return jax.shard_map(
        per_device, mesh=mesh, in_specs=in_specs, out_specs=out_specs, check_vma=False
    )
```
